32 devices in a mesh: groups: 2 (over y), ep: 4 (over z), role: 2 (over x), tp: 2 (over core).
Axes of the slice: x: 2, y: 2, z: 4, core: 2. Of those that a mesh axis runs over, the one named last changes fastest.
Arguments:
- moe_in: bfloat16 [128, 4096], P(('groups', 'ep', 'role'), 'tp'), parts along dimension 0, may hold values from -6 to 6
- expert_ids: int32 [128, 2], P(('groups', 'ep', 'role')), parts along dimension 0, may hold values from 0 to 3, all different within a row; in each aligned block of 8 rows (0 to 7, 8 to 15, ...) at most 6 rows name the same one
- gate_scores: float32 [128, 2], P(('groups', 'ep', 'role')), parts along dimension 0, may hold values from 0.05 to 0.5
- w_gate: bfloat16 [4, 4096, 1024], P('ep', 'tp', 'role'), may hold values from -0.09375 to 0.09375
- w_up: bfloat16 [4, 4096, 1024], P('ep', 'tp', 'role'), may hold values from -0.09375 to 0.09375
- w_down: bfloat16 [4, 1024, 4096], P('ep', None, ('role', 'tp')), may hold values from -0.1875 to 0.1875
- att_query: bfloat16 [64, 128, 576], P(('groups', 'ep', 'role'), 'tp'), parts along dimension 0, may hold values from -60 to 60
- att_cache: bfloat16 [64, 128, 576], P(('groups', 'ep', 'role')), parts along dimension 0, may hold values from -6 to 6
- cache_len: int32 [64], P(('groups', 'ep', 'role')), parts along dimension 0, may hold values from 2 to 128
Outputs:
- moe_out: bfloat16 [128, 4096], P(('groups', 'ep', 'role', 'tp')), parts along dimension 0
- att_out: bfloat16 [64, 128, 512], P(('groups', 'ep', 'role'), 'tp'), parts along dimension 0
The draws below stay inside these ranges and needn't reach their ends.
There are 2 independent parts, one for each index of `groups`. The reference program is written for one: setup_inputs(seed, part) draws one part's arguments, and reference() takes and returns one part's arrays. A program takes and returns all parts, laid end to end along the dimension named above; an argument that names none is the same for every part. Nothing has to cross between parts.
Inputs may be any that keep to these rules, and one draw needn't show every extreme that they name: `expert_ids`: each row names 2 different experts; in each aligned block of 8 rows (the rows of one device along ep and role) no expert is named more than 6 times, a bound that some block reaches.
All inputs are finite; a program needn't handle non-finite values.
Results may differ from the reference program's by a relative error of at most 0.0085.
Values may be sent and summed in bfloat16 or wider, within the bound.
A program may use at most 64 MiB of HBM per device.

```python
import math
import jax
import jax.numpy as jnp
import numpy as np
from jax import lax

D = 4096
FF = 1024
HEADS = 128
LAT = 512
ROPE = 64
ROW_DEV = 8
LEN = 128
EXPERTS = 4
TOPK = 2
CAP = 6
ROWS = 64
ATT_ROWS = 32
N_EP = 4
N_ROLE = 2


def cache_normal(key):
    return jnp.clip(jax.random.normal(key, (ATT_ROWS, LEN, LAT + ROPE), jnp.float32), -6.0, 6.0)


def draw_att_cache(key, part):
    base_field = cache_normal(key)
    return base_field.astype(jnp.bfloat16)


def draw_att_query(key, part):
    key = jax.random.fold_in(key, 9)
    queries = jnp.clip(jax.random.normal(key, (ATT_ROWS, HEADS, LAT + ROPE), jnp.float32), -6.0, 6.0)
    return queries.astype(jnp.bfloat16)


def place_ends(values, rng, low, top_value):
    dims = values.shape
    spot = [jax.random.randint(jax.random.fold_in(rng, axis), (), 0, dims[axis]) for axis in range(len(dims))]
    values = values.at[tuple(spot)].set(low)
    longest = dims.index(max(dims))
    spot[longest] = (spot[longest] + 1) % dims[longest]
    return values.at[tuple(spot)].set(top_value)


def levels(own_key, extent, pieces, least, largest):
    level = 1.0
    for position, blocks in pieces:
        heights = jax.random.uniform(jax.random.fold_in(jax.random.fold_in(own_key, 6), position), (blocks,), jnp.float32, least / len(pieces), largest / len(pieces))
        level = level * jnp.repeat(jnp.exp(heights), extent[position] // blocks).reshape((-1,) + (1,) * (len(extent) - 1 - position))
    return level


def deal_out(own_key, own, number, rows, count, top, limit, slope):
    order = jax.random.permutation(own_key, count)
    heavy_load, common = shares(count, rows * top, limit, slope, True), shares(count, rows * top, limit, slope, False)
    places = jnp.arange(count)

    def named(tallies, rotation):
        used = int((tallies > 0).sum())
        fixed = max(1, used // 4)
        shifted = fixed + (places - fixed + rotation * (used - fixed)) % max(1, count - fixed)
        return jnp.zeros((count,), jnp.int32).at[order[jnp.where(places < fixed, places, shifted)]].set(jnp.asarray(tallies, jnp.int32))

    tallies = jnp.where(number % 4 == 0, named(heavy_load, number // 4), named(common, number - number // 4 - 1))
    mixed = jax.random.permutation(jax.random.fold_in(own, 3), count)
    giver, taker = mixed[0:count // 2 * 2:2], mixed[1:count // 2 * 2:2]
    slack = jnp.minimum(tallies[giver] - 1, limit - tallies[taker]) // 2
    slack = jnp.where((giver == order[0]) | (taker == order[0]) | (tallies[taker] == 0), 0, jnp.maximum(slack, 0))
    shifted = jax.random.randint(jax.random.fold_in(own, 4), (count // 2,), 0, 1 << 20) % (slack + 1)
    tallies = tallies.at[giver].add(-shifted).at[taker].add(shifted)
    labels = jnp.searchsorted(jnp.cumsum(tallies), jnp.arange(rows * top), side="right").astype(jnp.int32)
    table = labels.reshape(top, rows).T
    table = table[jax.random.permutation(jax.random.fold_in(own, 1), rows)]
    rotation = jax.random.randint(jax.random.fold_in(own, 2), (rows, 1), 0, top)
    return jnp.take_along_axis(table, (jnp.arange(top)[None, :] + rotation) % top, axis=1)


def shares(amount, total, bound, skew, full):
    portions = [(1 << 20) // math.isqrt(standing ** skew) + 1 for standing in range(1, amount + 1)]
    largest = bound if full else min(bound, max(-(-total // amount), total * portions[0] // sum(portions)))
    least = 1 if total - largest >= amount - 1 else 0
    given, rest = [largest] + [least] * (amount - 1), total - largest - least * (amount - 1)
    while rest > 0:
        free = [i for i in range(1, amount) if given[i] < largest] or [i for i in range(1, amount) if given[i] < bound]
        pool, budget = sum([portions[i] for i in free]), rest
        for i in free:
            more = min(bound - given[i], max(1, budget * portions[i] // pool), rest)
            given[i] = given[i] + more
            rest = rest - more
    return np.array(given)


def gaussian(key, shape, scale, most, shards=(), kind=jnp.bfloat16):
    values = scale * jax.random.normal(key, shape, jnp.float32)
    if shards:
        values = values * levels(key, shape, shards, -0.22, 0.18)
    return jnp.clip(values, -most, most).astype(kind)


def setup_inputs(seed: int = 0, part: int = 0) -> dict:
    key_of = jax.random.split(jax.random.key(seed), 10)
    part_keys = jax.random.split(jax.random.fold_in(key_of[9], part), 10)
    moe_in = gaussian(part_keys[0], (ROWS, D), 1.0, 6.0, ((0, 8), (1, 2)))
    expert_ids_keys = jax.random.split(jax.random.fold_in(part_keys[1], 1), ROWS // ROW_DEV)
    expert_ids_turns = jax.random.permutation(jax.random.fold_in(part_keys[1], 3), ROWS // ROW_DEV)
    expert_ids = jax.vmap(lambda own, number: deal_out(jax.random.fold_in(part_keys[1], 2), own, number, ROW_DEV, EXPERTS, TOPK, CAP, 2))(expert_ids_keys, expert_ids_turns).reshape((ROWS, TOPK))
    gate_scores = jnp.clip(jnp.exp(math.log(0.5) - 2.3025851 * jax.random.uniform(part_keys[2], (ROWS, TOPK), jnp.float32) ** levels(part_keys[2], (ROWS, TOPK), ((0, 8),), -0.2, 0.2)), 0.05, 0.5)
    w_gate = gaussian(key_of[3], (EXPERTS, D, FF), D ** -0.5, 0.09375, ((0, 4), (1, 2), (2, 2)))
    w_up = gaussian(key_of[4], (EXPERTS, D, FF), D ** -0.5, 0.09375, ((0, 4), (1, 2), (2, 2)))
    w_down = gaussian(key_of[5], (EXPERTS, FF, D), FF ** -0.5, 0.1875, ((0, 4), (2, 4)))
    att_query = draw_att_query(jax.random.fold_in(jax.random.fold_in(key_of[9], part), 71), part)
    att_cache = draw_att_cache(jax.random.fold_in(jax.random.fold_in(key_of[9], part), 71), part)
    cache_len = place_ends(jax.random.randint(part_keys[8], (ATT_ROWS,), 2, LEN + 1), jax.random.fold_in(part_keys[8], 1), 2, LEN).astype(jnp.int32)
    return dict(moe_in=moe_in, expert_ids=expert_ids, gate_scores=gate_scores, w_gate=w_gate, w_up=w_up, w_down=w_down, att_query=att_query, att_cache=att_cache, cache_len=cache_len)


score_scale = 192.0 ** -0.5


def slot_ranks(flat_ids):
    total_pairs = flat_ids.shape[0]
    matches = flat_ids[:, None] == flat_ids[None, :]
    indices = jnp.arange(total_pairs, dtype=jnp.int32)
    earlier = indices[None, :] < indices[:, None]
    return jnp.sum((matches & earlier).astype(jnp.int32), axis=1).astype(jnp.int32)


def latent_attention(queries, entries, lengths):
    scores = jnp.einsum('rhc,rlc->rhl', queries.astype(jnp.float32), entries.astype(jnp.float32)) * score_scale
    visible = jnp.arange(entries.shape[1], dtype=jnp.int32)[None, None, :] < lengths[:, None, None]
    scores = jnp.where(visible, scores, -1e30)
    highest = jnp.max(scores, axis=2, keepdims=True)
    weights = jnp.exp(scores - highest)
    chances = (weights / jnp.sum(weights, axis=2, keepdims=True)).astype(jnp.bfloat16)
    values = entries[:, :, :LAT]
    return jnp.einsum('rhl,rlc->rhc', chances.astype(jnp.float32), values.astype(jnp.float32)).astype(jnp.bfloat16)


def reference(moe_in, expert_ids, gate_scores, w_gate, w_up, w_down, att_query, att_cache, cache_len):
    block_count = N_EP * N_ROLE
    slot_count = EXPERTS * CAP
    flat_ids = expert_ids.reshape(block_count, ROW_DEV * TOPK)
    target = flat_ids * CAP + jax.vmap(slot_ranks)(flat_ids)
    slot_hits = (target[:, :, None] == jnp.arange(slot_count, dtype=jnp.int32)[None, None, :]).astype(jnp.float32)
    slot_hits = slot_hits.reshape(block_count, ROW_DEV, TOPK, slot_count)
    placement = jnp.sum(slot_hits, axis=2)
    weighting = jnp.sum(slot_hits * gate_scores.reshape(block_count, ROW_DEV, TOPK, 1).astype(jnp.float32), axis=2)
    tokens = moe_in.reshape(block_count, ROW_DEV, D).astype(jnp.float32)

    def one_expert(running, expert):
        selector = lax.dynamic_slice_in_dim(placement, expert * CAP, CAP, 2)
        gathered = jnp.einsum('bwc,bwd->bcd', selector, tokens).astype(jnp.bfloat16).reshape(block_count * CAP, D)
        gate_sum = jnp.dot(gathered, w_gate[expert], preferred_element_type=jnp.float32)
        up_sum = jnp.dot(gathered, w_up[expert], preferred_element_type=jnp.float32)
        hidden = (jax.nn.silu(gate_sum) * up_sum).astype(jnp.bfloat16)
        result = jnp.dot(hidden, w_down[expert], preferred_element_type=jnp.float32).astype(jnp.bfloat16)
        result = result.reshape(block_count, CAP, D)
        portion = lax.dynamic_slice_in_dim(weighting, expert * CAP, CAP, 2)
        return running + jnp.einsum('bwc,bcd->bwd', portion, result.astype(jnp.float32)), None

    running, _ = lax.scan(one_expert, jnp.zeros((block_count, ROW_DEV, D), jnp.float32), jnp.arange(EXPERTS, dtype=jnp.int32))
    moe_out = running.reshape(block_count * ROW_DEV, D).astype(jnp.bfloat16)
    att_out = latent_attention(att_query, att_cache, cache_len)
    return (moe_out, att_out)
```

```python
import functools

import jax
import jax.numpy as jnp
from jax import lax
from jax.experimental import pallas as pl
from jax.experimental.pallas import tpu as pltpu
from jax.sharding import PartitionSpec as P

LAT = 512
MESH = pl.DeviceIdType.MESH
score_scale = 192.0 ** (-0.5)


def body(
    sizes,
    x, ids, gates, wg, wu, wd, query, cache, lens,
    moe, att,
    rows, wgv, wuv, wdv, qv, cv, psend, precv, hid, outb, ret, attv, moev,
    load_sem, put_sem, d_send, d_recv, p_sem, h_send, h_recv, r_send, r_recv,
):
    n_ep, n_role, n_tp = sizes
    quad = n_role * n_tp
    blocks = n_ep * n_role
    total = blocks * n_tp
    ep, role, tp = lax.axis_index("ep"), lax.axis_index("role"), lax.axis_index("tp")
    me_block = ep * n_role + role
    me_quad = role * n_tp + tp
    me = me_block * n_tp + tp
    small = total <= 16
    row_dev, width = x.shape
    part = row_dev // n_tp
    half = wgv.shape[1] // n_tp
    att_rows = qv.shape[0]

    def peer(index):
        return {
            "ep": lax.div(index, quad),
            "role": lax.rem(lax.div(index, n_tp), n_role),
            "tp": lax.rem(index, n_tp),
        }

    def each(start, stop, step):
        def run(k, carry):
            step(k)
            return carry

        lax.fori_loop(start, stop, run, 0, unroll=small)

    barrier = pltpu.get_barrier_semaphore()

    def greet(k):
        pl.semaphore_signal(
            barrier, inc=1, device_id=peer(lax.rem(me + k, total)), device_id_type=MESH
        )

    each(1, total, greet)

    own = pltpu.make_async_copy(x, rows.at[me_block], load_sem.at[0])
    loads = [
        pltpu.make_async_copy(source, target, load_sem.at[1 + i])
        for i, (source, target) in enumerate(
            [(query, qv), (cache, cv), (wg, wgv), (wu, wuv), (wd, wdv)]
        )
    ]
    own.start()
    for load in loads:
        load.start()

    pl.semaphore_wait(barrier, total - 1)

    def dispatch(block, source):
        return pltpu.make_async_remote_copy(
            src_ref=x,
            dst_ref=rows.at[source],
            send_sem=d_send.at[block],
            recv_sem=d_recv.at[source],
            device_id=peer(block * n_tp + tp),
            device_id_type=MESH,
        )

    each(1, blocks, lambda k: dispatch(lax.rem(me_block + k, blocks), me_block).start())

    def attend(r):
        q, entries = qv[r], cv[r]
        scores = (
            jnp.dot(q, entries, preferred_element_type=jnp.float32) * score_scale
        )
        visible = lax.broadcasted_iota(jnp.int32, scores.shape, 1) < lens[r]
        scores = jnp.where(visible, scores, -1e30)
        weights = jnp.exp(scores - jnp.max(scores, axis=1, keepdims=True))
        chances = (weights / jnp.sum(weights, axis=1, keepdims=True)).astype(jnp.bfloat16)
        attv[r] = lax.dot_general(
            chances, entries[:LAT], (((1,), (1,)), ((), ())), preferred_element_type=jnp.float32
        ).astype(jnp.bfloat16)

    def put(r):
        return pltpu.make_async_copy(attv.at[r], att.at[r], put_sem.at[r])

    loads[0].wait()
    loads[1].wait()
    cut = att_rows // 2
    for r in range(cut):
        attend(r)
        put(r).start()

    loads[2].wait()
    loads[3].wait()
    own.wait()
    each(1, blocks, lambda k: dispatch(me_block, lax.rem(me_block + k, blocks)).wait_recv())

    gathered = (
        rows[...].astype(jnp.float32).reshape(blocks * row_dev, width).astype(jnp.bfloat16)
    )

    def column_sums(which):
        columns = pl.ds(pl.multiple_of(which * half, half), half)
        gate = jnp.dot(gathered, wgv[:, columns], preferred_element_type=jnp.float32)
        up = jnp.dot(gathered, wuv[:, columns], preferred_element_type=jnp.float32)
        return gate, up

    gate, up = column_sums(1 - tp)
    psend[0] = gate
    psend[1] = up
    swap = pltpu.make_async_remote_copy(
        src_ref=psend,
        dst_ref=precv,
        send_sem=p_sem.at[0],
        recv_sem=p_sem.at[1],
        device_id={"tp": 1 - tp},
        device_id_type=MESH,
    )
    swap.start()
    gate, up = column_sums(tp)
    swap.wait_recv()
    gate = gate + precv[0]
    up = up + precv[1]
    hid[me_quad] = (gate / (1.0 + jnp.exp(-gate)) * up).astype(jnp.bfloat16)

    def share(target, source):
        return pltpu.make_async_remote_copy(
            src_ref=hid.at[me_quad],
            dst_ref=hid.at[source],
            send_sem=h_send.at[target],
            recv_sem=h_recv.at[source],
            device_id={"role": lax.div(target, n_tp), "tp": lax.rem(target, n_tp)},
            device_id_type=MESH,
        )

    for k in range(1, quad):
        share(lax.rem(me_quad + k, quad), me_quad).start()

    for r in range(cut, att_rows):
        attend(r)
        put(r).start()

    loads[4].wait()
    produced = None
    for k in range(quad):
        source = lax.rem(me_quad + k, quad)
        if k:
            share(me_quad, source).wait_recv()
        span = pl.ds(pl.multiple_of(source * half, half), half)
        term = jnp.dot(hid[source], wdv[span, :], preferred_element_type=jnp.float32)
        produced = term if produced is None else produced + term

    outb[...] = produced.reshape(total, part, produced.shape[1]).astype(jnp.bfloat16)

    def give(target, source):
        return pltpu.make_async_remote_copy(
            src_ref=outb.at[target],
            dst_ref=ret.at[source],
            send_sem=r_send.at[target],
            recv_sem=r_recv.at[source],
            device_id=peer(target),
            device_id_type=MESH,
        )

    each(1, total, lambda k: give(lax.rem(me + k, total), me).start())
    keep = pltpu.make_async_copy(outb.at[me], ret.at[me], load_sem.at[0])
    keep.start()

    named, score = ids[...], gates[...]
    mine = lax.broadcasted_iota(jnp.int32, (part, row_dev), 1) == tp * part + (
        lax.broadcasted_iota(jnp.int32, (part, row_dev), 0)
    )
    table = []
    for e in range(n_ep):
        weight = jnp.sum(jnp.where(named == e, score, 0.0), axis=0, keepdims=True)
        table.append(jnp.sum(jnp.where(mine, weight, 0.0), axis=1, keepdims=True))

    keep.wait()
    each(1, total, lambda k: give(me, lax.rem(me + k, total)).wait_recv())

    columns = ret.shape[2]
    for j in range(quad):
        acc = None
        for e in range(n_ep):
            term = table[e] * ret[e * quad + j].astype(jnp.float32)
            acc = term if acc is None else acc + term
        moev[:, j * columns : (j + 1) * columns] = acc.astype(jnp.bfloat16)
    last = pltpu.make_async_copy(moev, moe, load_sem.at[1])
    last.start()

    each(1, blocks, lambda k: dispatch(lax.rem(me_block + k, blocks), me_block).wait_send())
    swap.wait_send()
    for k in range(1, quad):
        share(lax.rem(me_quad + k, quad), me_quad).wait_send()
    each(1, total, lambda k: give(lax.rem(me + k, total), me).wait_send())
    for r in range(att_rows):
        put(r).wait()
    last.wait()


def shards(sizes, moe_in, expert_ids, gate_scores, w_gate, w_up, w_down, att_query, att_cache, cache_len):
    n_ep, n_role, n_tp = sizes
    quad, blocks = n_role * n_tp, n_ep * n_role
    total = blocks * n_tp
    row_dev, width = moe_in.shape
    part = row_dev // n_tp
    hidden = w_gate.shape[2]
    units, columns = w_down.shape[1:]
    half = hidden // n_tp
    att_rows, heads, _ = att_query.shape
    entries = jnp.swapaxes(att_cache, 1, 2)
    bf16, f32 = jnp.bfloat16, jnp.float32
    anywhere = pl.BlockSpec(memory_space=pl.ANY)
    vmem = pl.BlockSpec(memory_space=pltpu.VMEM)
    smem = pl.BlockSpec(memory_space=pltpu.SMEM)
    dma = pltpu.SemaphoreType.DMA
    flops = 2 * blocks * row_dev * (2 * width * hidden + units * columns)
    return pl.pallas_call(
        functools.partial(body, sizes),
        out_shape=(
            jax.ShapeDtypeStruct((part, columns * quad), bf16),
            jax.ShapeDtypeStruct((att_rows, heads, LAT), bf16),
        ),
        in_specs=[anywhere, vmem, vmem] + [anywhere] * 5 + [smem],
        out_specs=(anywhere, anywhere),
        scratch_shapes=[
            pltpu.VMEM((blocks, row_dev, width), bf16),
            pltpu.VMEM((width, hidden), bf16),
            pltpu.VMEM((width, hidden), bf16),
            pltpu.VMEM((units, columns), bf16),
            pltpu.VMEM(att_query.shape, bf16),
            pltpu.VMEM(entries.shape, bf16),
            pltpu.VMEM((2, blocks * row_dev, half), f32),
            pltpu.VMEM((2, blocks * row_dev, half), f32),
            pltpu.VMEM((quad, blocks * row_dev, half), bf16),
            pltpu.VMEM((total, part, columns), bf16),
            pltpu.VMEM((total, part, columns), bf16),
            pltpu.VMEM((att_rows, heads, LAT), bf16),
            pltpu.VMEM((part, columns * quad), bf16),
            dma((6,)),
            dma((att_rows,)),
            dma((blocks,)),
            dma((blocks,)),
            dma((2,)),
            dma((quad,)),
            dma((quad,)),
            dma((total,)),
            dma((total,)),
        ],
        compiler_params=pltpu.CompilerParams(
            collective_id=0, has_side_effects=True, vmem_limit_bytes=56 * 1024 * 1024
        ),
        cost_estimate=pl.CostEstimate(flops=flops, bytes_accessed=8 << 20, transcendentals=0),
    )(
        moe_in, expert_ids.T, gate_scores.T, w_gate[0], w_up[0], w_down[0], att_query, entries, cache_len
    )


def solution(mesh):
    placed = (
        P(("groups", "ep", "role"), "tp"),
        P(("groups", "ep", "role"), None),
        P(("groups", "ep", "role"), None),
        P("ep", "tp", "role"),
        P("ep", "tp", "role"),
        P("ep", None, ("role", "tp")),
        P(("groups", "ep", "role"), "tp", None),
        P(("groups", "ep", "role"), None, None),
        P(("groups", "ep", "role")),
    )
    sizes = (mesh.shape["ep"], mesh.shape["role"], mesh.shape["tp"])
    return jax.shard_map(
        functools.partial(shards, sizes),
        mesh=mesh,
        in_specs=placed,
        out_specs=(
            P(("groups", "ep", "role", "tp"), None),
            P(("groups", "ep", "role"), "tp", None),
        ),
        check_vma=False,
    )
```

```python
import functools

import jax
import jax.numpy as jnp
from jax import lax
from jax.experimental import pallas as pl
from jax.experimental.pallas import tpu as pltpu
from jax.sharding import PartitionSpec as P

LAT = 512
MESH = pl.DeviceIdType.MESH
score_scale = 192.0 ** (-0.5)


def body(
    sizes,
    x, ids, gates, wg, wu, wd, query, cache, lens,
    moe, att,
    rows, wgv, wuv, wdv, qv, cv, psend, precv, hid, outb, ret, attv, moev,
    load_sem, put_sem, d_send, d_recv, p_sem, h_send, h_recv, r_send, r_recv,
):
    n_ep, n_role, n_tp = sizes
    quad = n_role * n_tp
    blocks = n_ep * n_role
    total = blocks * n_tp
    ep, role, tp = lax.axis_index("ep"), lax.axis_index("role"), lax.axis_index("tp")
    me_block = ep * n_role + role
    me_quad = role * n_tp + tp
    me = me_block * n_tp + tp
    small = total <= 16
    row_dev, width = x.shape
    part = row_dev // n_tp
    half = wgv.shape[1] // n_tp
    att_rows = qv.shape[0]

    def peer(index):
        return {
            "ep": lax.div(index, quad),
            "role": lax.rem(lax.div(index, n_tp), n_role),
            "tp": lax.rem(index, n_tp),
        }

    def each(start, stop, step):
        def run(k, carry):
            step(k)
            return carry

        lax.fori_loop(start, stop, run, 0, unroll=small)

    barrier = pltpu.get_barrier_semaphore()

    def greet(k):
        pl.semaphore_signal(
            barrier, inc=1, device_id=peer(lax.rem(me + k, total)), device_id_type=MESH
        )

    each(1, total, greet)

    own = pltpu.make_async_copy(x, rows.at[me_block], load_sem.at[0])
    loads = [
        pltpu.make_async_copy(source, target, load_sem.at[1 + i])
        for i, (source, target) in enumerate(
            [(query, qv), (cache, cv), (wg, wgv), (wu, wuv), (wd, wdv)]
        )
    ]
    own.start()
    for load in loads:
        load.start()

    pl.semaphore_wait(barrier, total - 1)

    def dispatch(block, source):
        return pltpu.make_async_remote_copy(
            src_ref=x,
            dst_ref=rows.at[source],
            send_sem=d_send.at[block],
            recv_sem=d_recv.at[source],
            device_id=peer(block * n_tp + tp),
            device_id_type=MESH,
        )

    each(1, blocks, lambda k: dispatch(lax.rem(me_block + k, blocks), me_block).start())

    def attend(r):
        q, entries = qv[r], cv[r]
        scores = (
            jnp.dot(q, entries, preferred_element_type=jnp.float32) * score_scale
        )
        visible = lax.broadcasted_iota(jnp.int32, scores.shape, 1) < lens[r]
        scores = jnp.where(visible, scores, -1e30)
        weights = jnp.exp(scores - jnp.max(scores, axis=1, keepdims=True))
        chances = (weights / jnp.sum(weights, axis=1, keepdims=True)).astype(jnp.bfloat16)
        attv[r] = lax.dot_general(
            chances, entries[:LAT], (((1,), (1,)), ((), ())), preferred_element_type=jnp.float32
        ).astype(jnp.bfloat16)

    def put(r):
        return pltpu.make_async_copy(attv.at[r], att.at[r], put_sem.at[r])

    loads[0].wait()
    loads[1].wait()
    cut = att_rows // 2
    for r in range(cut):
        attend(r)
        put(r).start()

    loads[2].wait()
    loads[3].wait()
    own.wait()
    each(1, blocks, lambda k: dispatch(me_block, lax.rem(me_block + k, blocks)).wait_recv())

    gathered = (
        rows[...].astype(jnp.float32).reshape(blocks * row_dev, width).astype(jnp.bfloat16)
    )

    def column_sums(which):
        columns = pl.ds(pl.multiple_of(which * half, half), half)
        gate = jnp.dot(gathered, wgv[:, columns], preferred_element_type=jnp.float32)
        up = jnp.dot(gathered, wuv[:, columns], preferred_element_type=jnp.float32)
        return gate, up

    gate, up = column_sums(1 - tp)
    psend[0] = gate
    psend[1] = up
    swap = pltpu.make_async_remote_copy(
        src_ref=psend,
        dst_ref=precv,
        send_sem=p_sem.at[0],
        recv_sem=p_sem.at[1],
        device_id={"tp": 1 - tp},
        device_id_type=MESH,
    )
    swap.start()
    gate, up = column_sums(tp)
    swap.wait_recv()
    gate = gate + precv[0]
    up = up + precv[1]
    hid[me_quad] = (gate / (1.0 + jnp.exp(-gate)) * up).astype(jnp.bfloat16)

    def share(target, source):
        return pltpu.make_async_remote_copy(
            src_ref=hid.at[me_quad],
            dst_ref=hid.at[source],
            send_sem=h_send.at[target],
            recv_sem=h_recv.at[source],
            device_id={"role": lax.div(target, n_tp), "tp": lax.rem(target, n_tp)},
            device_id_type=MESH,
        )

    for k in range(1, quad):
        share(lax.rem(me_quad + k, quad), me_quad).start()

    for r in range(cut, att_rows):
        attend(r)
        put(r).start()

    loads[4].wait()
    produced = None
    for k in range(quad):
        source = lax.rem(me_quad + k, quad)
        if k:
            share(me_quad, source).wait_recv()
        span = pl.ds(pl.multiple_of(source * half, half), half)
        term = jnp.dot(hid[source], wdv[span, :], preferred_element_type=jnp.float32)
        produced = term if produced is None else produced + term

    outb[...] = produced.reshape(total, part, produced.shape[1]).astype(jnp.bfloat16)

    def give(target, source):
        return pltpu.make_async_remote_copy(
            src_ref=outb.at[target],
            dst_ref=ret.at[source],
            send_sem=r_send.at[target],
            recv_sem=r_recv.at[source],
            device_id=peer(target),
            device_id_type=MESH,
        )

    each(1, total, lambda k: give(lax.rem(me + k, total), me).start())
    keep = pltpu.make_async_copy(outb.at[me], ret.at[me], load_sem.at[0])
    keep.start()

    named, score = ids[...], gates[...]
    mine = lax.broadcasted_iota(jnp.int32, (part, row_dev), 1) == tp * part + (
        lax.broadcasted_iota(jnp.int32, (part, row_dev), 0)
    )
    table = []
    for e in range(n_ep):
        weight = jnp.sum(jnp.where(named == e, score, 0.0), axis=0, keepdims=True)
        table.append(jnp.sum(jnp.where(mine, weight, 0.0), axis=1, keepdims=True))

    keep.wait()
    each(1, total, lambda k: give(me, lax.rem(me + k, total)).wait_recv())

    columns = ret.shape[2]
    for j in range(quad):
        acc = None
        for e in range(n_ep):
            term = table[e] * ret[e * quad + j].astype(jnp.float32)
            acc = term if acc is None else acc + term
        moev[:, j * columns : (j + 1) * columns] = acc.astype(jnp.bfloat16)
    last = pltpu.make_async_copy(moev, moe, load_sem.at[1])
    last.start()

    each(1, blocks, lambda k: dispatch(lax.rem(me_block + k, blocks), me_block).wait_send())
    swap.wait_send()
    for k in range(1, quad):
        share(lax.rem(me_quad + k, quad), me_quad).wait_send()
    each(1, total, lambda k: give(lax.rem(me + k, total), me).wait_send())
    for r in range(att_rows):
        put(r).wait()
    last.wait()


def shards(sizes, moe_in, expert_ids, gate_scores, w_gate, w_up, w_down, att_query, att_cache, cache_len):
    n_ep, n_role, n_tp = sizes
    quad, blocks = n_role * n_tp, n_ep * n_role
    total = blocks * n_tp
    row_dev, width = moe_in.shape
    part = row_dev // n_tp
    hidden = w_gate.shape[2]
    units, columns = w_down.shape[1:]
    half = hidden // n_tp
    att_rows, heads, _ = att_query.shape
    entries = jnp.swapaxes(att_cache, 1, 2)
    bf16, f32 = jnp.bfloat16, jnp.float32
    anywhere = pl.BlockSpec(memory_space=pl.ANY)
    vmem = pl.BlockSpec(memory_space=pltpu.VMEM)
    smem = pl.BlockSpec(memory_space=pltpu.SMEM)
    dma = pltpu.SemaphoreType.DMA
    flops = 2 * blocks * row_dev * (2 * width * hidden + units * columns)
    moe, att = pl.pallas_call(
        functools.partial(body, sizes),
        out_shape=(
            jax.ShapeDtypeStruct((part, columns * quad), bf16),
            jax.ShapeDtypeStruct((att_rows, heads, LAT), bf16),
        ),
        in_specs=[anywhere, vmem, vmem] + [anywhere] * 5 + [smem],
        out_specs=(anywhere, anywhere),
        scratch_shapes=[
            pltpu.VMEM((blocks, row_dev, width), bf16),
            pltpu.VMEM((width, hidden), bf16),
            pltpu.VMEM((width, hidden), bf16),
            pltpu.VMEM((units, columns), bf16),
            pltpu.VMEM(att_query.shape, bf16),
            pltpu.VMEM(entries.shape, bf16),
            pltpu.VMEM((2, blocks * row_dev, half), f32),
            pltpu.VMEM((2, blocks * row_dev, half), f32),
            pltpu.VMEM((quad, blocks * row_dev, half), bf16),
            pltpu.VMEM((total, part, columns), bf16),
            pltpu.VMEM((total, part, columns), bf16),
            pltpu.VMEM((att_rows, heads, LAT), bf16),
            pltpu.VMEM((part, columns * quad), bf16),
            dma((6,)),
            dma((att_rows,)),
            dma((blocks,)),
            dma((blocks,)),
            dma((2,)),
            dma((quad,)),
            dma((quad,)),
            dma((total,)),
            dma((total,)),
        ],
        compiler_params=pltpu.CompilerParams(
            collective_id=0, has_side_effects=True, vmem_limit_bytes=56 * 1024 * 1024
        ),
        cost_estimate=pl.CostEstimate(flops=flops, bytes_accessed=8 << 20, transcendentals=0),
    )(
        moe_in, expert_ids.T, gate_scores.T, w_gate[0], w_up[0], w_down[0], att_query, entries, cache_len
    )
    return settled(moe, att, pltpu.VMEM)


def settle(a, b, out_a, out_b, sem):
    first = pltpu.make_async_copy(a, out_a, sem.at[0])
    second = pltpu.make_async_copy(b, out_b, sem.at[1])
    second.start()
    first.start()
    second.wait()
    first.wait()


def settled(a, b, space):
    anywhere = pl.BlockSpec(memory_space=pl.ANY)
    inner = pl.BlockSpec(memory_space=space)
    return pl.pallas_call(
        settle,
        out_shape=(jax.ShapeDtypeStruct(a.shape, a.dtype), jax.ShapeDtypeStruct(b.shape, b.dtype)),
        in_specs=[inner, inner],
        out_specs=(anywhere, anywhere),
        scratch_shapes=[pltpu.SemaphoreType.DMA((2,))],
    )(a, b)


def solution(mesh):
    placed = (
        P(("groups", "ep", "role"), "tp"),
        P(("groups", "ep", "role"), None),
        P(("groups", "ep", "role"), None),
        P("ep", "tp", "role"),
        P("ep", "tp", "role"),
        P("ep", None, ("role", "tp")),
        P(("groups", "ep", "role"), "tp", None),
        P(("groups", "ep", "role"), None, None),
        P(("groups", "ep", "role")),
    )
    sizes = (mesh.shape["ep"], mesh.shape["role"], mesh.shape["tp"])
    return jax.shard_map(
        functools.partial(shards, sizes),
        mesh=mesh,
        in_specs=placed,
        out_specs=(
            P(("groups", "ep", "role", "tp"), None),
            P(("groups", "ep", "role"), "tp", None),
        ),
        check_vma=False,
    )
```

```python
import functools

import jax
import jax.numpy as jnp
from jax import lax
from jax.experimental import pallas as pl
from jax.experimental.pallas import tpu as pltpu
from jax.sharding import PartitionSpec as P

LAT = 512
MESH = pl.DeviceIdType.MESH
score_scale = 192.0 ** (-0.5)


def body(
    sizes,
    x, ids, gates, wg, wu, wd, query, cache, lens,
    moe, att,
    rows, wgv, wuv, wdv, qv, cv, psend, precv, hid, outb, ret, attv, moev,
    load_sem, put_sem, d_send, d_recv, f_send, p_sem, h_send, h_recv, r_send, r_recv,
):
    n_ep, n_role, n_tp = sizes
    quad = n_role * n_tp
    blocks = n_ep * n_role
    total = blocks * n_tp
    ep, role, tp = lax.axis_index("ep"), lax.axis_index("role"), lax.axis_index("tp")
    me_block = ep * n_role + role
    me_quad = role * n_tp + tp
    me = me_block * n_tp + tp
    small = total <= 16
    row_dev, width = x.shape
    part = row_dev // n_tp
    half = wgv.shape[1] // n_tp
    att_rows = qv.shape[0]

    def peer(index):
        return {
            "ep": lax.div(index, quad),
            "role": lax.rem(lax.div(index, n_tp), n_role),
            "tp": lax.rem(index, n_tp),
        }

    def each(start, stop, step):
        def run(k, carry):
            step(k)
            return carry

        lax.fori_loop(start, stop, run, 0, unroll=small)

    barrier = pltpu.get_barrier_semaphore()

    def greet(k):
        pl.semaphore_signal(
            barrier, inc=1, device_id=peer(lax.rem(me + k, total)), device_id_type=MESH
        )

    each(1, total, greet)

    own = pltpu.make_async_copy(x, rows.at[me_block], load_sem.at[0])
    loads = [
        pltpu.make_async_copy(source, target, load_sem.at[1 + i])
        for i, (source, target) in enumerate(
            [(query, qv), (cache, cv), (wg, wgv), (wu, wuv), (wd, wdv)]
        )
    ]
    own.start()
    for load in loads:
        load.start()

    own.wait()
    pl.semaphore_wait(barrier, total - 1)

    def dispatch(block, source):
        return pltpu.make_async_remote_copy(
            src_ref=rows.at[me_block],
            dst_ref=rows.at[source],
            send_sem=d_send.at[block],
            recv_sem=d_recv.at[source],
            device_id=peer(block * n_tp + tp),
            device_id_type=MESH,
        )

    half_ep = n_ep // 2
    near = lax.div(ep, half_ep) * half_ep
    far = lax.rem(near + half_ep, n_ep)

    def near_block(k):
        return near * n_role + lax.rem(me_block - near * n_role + k, half_ep * n_role)

    def far_ep(k):
        return far + lax.rem(ep - near + k, half_ep)

    def relay(source_ep, target, j):
        block = source_ep * n_role + lax.rem(role + j, n_role) if j else source_ep * n_role + role
        return pltpu.make_async_remote_copy(
            src_ref=rows.at[block],
            dst_ref=rows.at[block],
            send_sem=f_send.at[source_ep * n_role + target],
            recv_sem=d_recv.at[block],
            device_id={"role": target},
            device_id_type=MESH,
        )

    each(0, half_ep, lambda k: dispatch(far_ep(k) * n_role + role, me_block).start())
    each(1, half_ep * n_role, lambda k: dispatch(near_block(k), me_block).start())

    def pass_on(k):
        source = far_ep(k)
        dispatch(me_block, source * n_role + role).wait_recv()
        for j in range(1, n_role):
            relay(source, lax.rem(role + j, n_role), 0).start()

    def attend(r):
        q, entries = qv[r], cv[r]
        scores = (
            jnp.dot(q, entries, preferred_element_type=jnp.float32) * score_scale
        )
        visible = lax.broadcasted_iota(jnp.int32, scores.shape, 1) < lens[r]
        scores = jnp.where(visible, scores, -1e30)
        weights = jnp.exp(scores - jnp.max(scores, axis=1, keepdims=True))
        chances = (weights / jnp.sum(weights, axis=1, keepdims=True)).astype(jnp.bfloat16)
        attv[r] = lax.dot_general(
            chances, entries[:LAT], (((1,), (1,)), ((), ())), preferred_element_type=jnp.float32
        ).astype(jnp.bfloat16)

    def put(r):
        return pltpu.make_async_copy(attv.at[r], att.at[r], put_sem.at[r])

    loads[0].wait()
    loads[1].wait()
    cut = att_rows // 2
    for r in range(cut):
        attend(r)
        put(r).start()
        if r == 0:
            each(0, half_ep, pass_on)

    loads[2].wait()
    loads[3].wait()
    each(1, half_ep * n_role, lambda k: dispatch(me_block, near_block(k)).wait_recv())

    def relayed(k):
        for j in range(1, n_role):
            relay(far_ep(k), role, j).wait_recv()

    each(0, half_ep, relayed)

    gathered = (
        rows[...].astype(jnp.float32).reshape(blocks * row_dev, width).astype(jnp.bfloat16)
    )

    def column_sums(which):
        columns = pl.ds(pl.multiple_of(which * half, half), half)
        gate = jnp.dot(gathered, wgv[:, columns], preferred_element_type=jnp.float32)
        up = jnp.dot(gathered, wuv[:, columns], preferred_element_type=jnp.float32)
        return gate, up

    gate, up = column_sums(1 - tp)
    psend[0] = gate
    psend[1] = up
    swap = pltpu.make_async_remote_copy(
        src_ref=psend,
        dst_ref=precv,
        send_sem=p_sem.at[0],
        recv_sem=p_sem.at[1],
        device_id={"tp": 1 - tp},
        device_id_type=MESH,
    )
    swap.start()
    gate, up = column_sums(tp)
    swap.wait_recv()
    gate = gate + precv[0]
    up = up + precv[1]
    hid[me_quad] = (gate / (1.0 + jnp.exp(-gate)) * up).astype(jnp.bfloat16)

    def share(target, source):
        return pltpu.make_async_remote_copy(
            src_ref=hid.at[me_quad],
            dst_ref=hid.at[source],
            send_sem=h_send.at[target],
            recv_sem=h_recv.at[source],
            device_id={"role": lax.div(target, n_tp), "tp": lax.rem(target, n_tp)},
            device_id_type=MESH,
        )

    for k in range(1, quad):
        share(lax.rem(me_quad + k, quad), me_quad).start()

    for r in range(cut, att_rows):
        attend(r)
        put(r).start()

    loads[4].wait()
    produced = None
    for k in range(quad):
        source = lax.rem(me_quad + k, quad)
        if k:
            share(me_quad, source).wait_recv()
        span = pl.ds(pl.multiple_of(source * half, half), half)
        term = jnp.dot(hid[source], wdv[span, :], preferred_element_type=jnp.float32)
        produced = term if produced is None else produced + term

    outb[...] = produced.reshape(total, part, produced.shape[1]).astype(jnp.bfloat16)

    def give(target, source):
        return pltpu.make_async_remote_copy(
            src_ref=outb.at[target],
            dst_ref=ret.at[source],
            send_sem=r_send.at[target],
            recv_sem=r_recv.at[source],
            device_id=peer(target),
            device_id_type=MESH,
        )

    each(1, total, lambda k: give(lax.rem(me + k, total), me).start())
    keep = pltpu.make_async_copy(outb.at[me], ret.at[me], load_sem.at[0])
    keep.start()

    named, score = ids[...], gates[...]
    mine = lax.broadcasted_iota(jnp.int32, (part, row_dev), 1) == tp * part + (
        lax.broadcasted_iota(jnp.int32, (part, row_dev), 0)
    )
    table = []
    for e in range(n_ep):
        weight = jnp.sum(jnp.where(named == e, score, 0.0), axis=0, keepdims=True)
        table.append(jnp.sum(jnp.where(mine, weight, 0.0), axis=1, keepdims=True))

    keep.wait()
    each(1, total, lambda k: give(me, lax.rem(me + k, total)).wait_recv())

    columns = ret.shape[2]
    for j in range(quad):
        acc = None
        for e in range(n_ep):
            term = table[e] * ret[e * quad + j].astype(jnp.float32)
            acc = term if acc is None else acc + term
        moev[:, j * columns : (j + 1) * columns] = acc.astype(jnp.bfloat16)
    last = pltpu.make_async_copy(moev, moe, load_sem.at[1])
    last.start()

    each(0, half_ep, lambda k: dispatch(far_ep(k) * n_role + role, me_block).wait_send())
    each(1, half_ep * n_role, lambda k: dispatch(near_block(k), me_block).wait_send())

    def sent(k):
        for j in range(1, n_role):
            relay(far_ep(k), lax.rem(role + j, n_role), 0).wait_send()

    each(0, half_ep, sent)
    swap.wait_send()
    for k in range(1, quad):
        share(lax.rem(me_quad + k, quad), me_quad).wait_send()
    each(1, total, lambda k: give(lax.rem(me + k, total), me).wait_send())
    for r in range(att_rows):
        put(r).wait()
    last.wait()


def shards(sizes, moe_in, expert_ids, gate_scores, w_gate, w_up, w_down, att_query, att_cache, cache_len):
    n_ep, n_role, n_tp = sizes
    quad, blocks = n_role * n_tp, n_ep * n_role
    total = blocks * n_tp
    row_dev, width = moe_in.shape
    part = row_dev // n_tp
    hidden = w_gate.shape[2]
    units, columns = w_down.shape[1:]
    half = hidden // n_tp
    att_rows, heads, _ = att_query.shape
    entries = jnp.swapaxes(att_cache, 1, 2)
    bf16, f32 = jnp.bfloat16, jnp.float32
    anywhere = pl.BlockSpec(memory_space=pl.ANY)
    vmem = pl.BlockSpec(memory_space=pltpu.VMEM)
    smem = pl.BlockSpec(memory_space=pltpu.SMEM)
    dma = pltpu.SemaphoreType.DMA
    flops = 2 * blocks * row_dev * (2 * width * hidden + units * columns)
    moe, att = pl.pallas_call(
        functools.partial(body, sizes),
        out_shape=(
            jax.ShapeDtypeStruct((part, columns * quad), bf16),
            jax.ShapeDtypeStruct((att_rows, heads, LAT), bf16),
        ),
        in_specs=[anywhere, vmem, vmem] + [anywhere] * 5 + [smem],
        out_specs=(anywhere, anywhere),
        scratch_shapes=[
            pltpu.VMEM((blocks, row_dev, width), bf16),
            pltpu.VMEM((width, hidden), bf16),
            pltpu.VMEM((width, hidden), bf16),
            pltpu.VMEM((units, columns), bf16),
            pltpu.VMEM(att_query.shape, bf16),
            pltpu.VMEM(entries.shape, bf16),
            pltpu.VMEM((2, blocks * row_dev, half), f32),
            pltpu.VMEM((2, blocks * row_dev, half), f32),
            pltpu.VMEM((quad, blocks * row_dev, half), bf16),
            pltpu.VMEM((total, part, columns), bf16),
            pltpu.VMEM((total, part, columns), bf16),
            pltpu.VMEM((att_rows, heads, LAT), bf16),
            pltpu.VMEM((part, columns * quad), bf16),
            dma((6,)),
            dma((att_rows,)),
            dma((blocks,)),
            dma((blocks,)),
            dma((blocks,)),
            dma((2,)),
            dma((quad,)),
            dma((quad,)),
            dma((total,)),
            dma((total,)),
        ],
        compiler_params=pltpu.CompilerParams(
            collective_id=0, has_side_effects=True, vmem_limit_bytes=56 * 1024 * 1024
        ),
        cost_estimate=pl.CostEstimate(flops=flops, bytes_accessed=8 << 20, transcendentals=0),
    )(
        moe_in, expert_ids.T, gate_scores.T, w_gate[0], w_up[0], w_down[0], att_query, entries, cache_len
    )
    return settled(moe, att, pltpu.VMEM)


def settle(a, b, out_a, out_b, sem):
    first = pltpu.make_async_copy(a, out_a, sem.at[0])
    second = pltpu.make_async_copy(b, out_b, sem.at[1])
    second.start()
    first.start()
    second.wait()
    first.wait()


def settled(a, b, space):
    anywhere = pl.BlockSpec(memory_space=pl.ANY)
    inner = pl.BlockSpec(memory_space=space)
    return pl.pallas_call(
        settle,
        out_shape=(jax.ShapeDtypeStruct(a.shape, a.dtype), jax.ShapeDtypeStruct(b.shape, b.dtype)),
        in_specs=[inner, inner],
        out_specs=(anywhere, anywhere),
        scratch_shapes=[pltpu.SemaphoreType.DMA((2,))],
    )(a, b)


def solution(mesh):
    placed = (
        P(("groups", "ep", "role"), "tp"),
        P(("groups", "ep", "role"), None),
        P(("groups", "ep", "role"), None),
        P("ep", "tp", "role"),
        P("ep", "tp", "role"),
        P("ep", None, ("role", "tp")),
        P(("groups", "ep", "role"), "tp", None),
        P(("groups", "ep", "role"), None, None),
        P(("groups", "ep", "role")),
    )
    sizes = (mesh.shape["ep"], mesh.shape["role"], mesh.shape["tp"])
    return jax.shard_map(
        functools.partial(shards, sizes),
        mesh=mesh,
        in_specs=placed,
        out_specs=(
            P(("groups", "ep", "role", "tp"), None),
            P(("groups", "ep", "role"), "tp", None),
        ),
        check_vma=False,
    )
```

```python
import functools

import jax
import jax.numpy as jnp
from jax import lax
from jax.experimental import pallas as pl
from jax.experimental.pallas import tpu as pltpu
from jax.sharding import PartitionSpec as P

LAT = 512
MESH = pl.DeviceIdType.MESH
score_scale = 192.0 ** (-0.5)


def body(
    sizes,
    x, ids, gates, wg, wu, wd, query, cache, lens,
    moe, att,
    rows, wgv, wuv, wdv, qv, cv, psend, precv, hid, outb, ret, attv, moev,
    load_sem, put_sem, d_send, d_recv, f_send, p_sem, h_send, h_recv, r_send, r_recv,
):
    n_ep, n_role, n_tp = sizes
    quad = n_role * n_tp
    blocks = n_ep * n_role
    total = blocks * n_tp
    ep, role, tp = lax.axis_index("ep"), lax.axis_index("role"), lax.axis_index("tp")
    me_block = ep * n_role + role
    me_quad = role * n_tp + tp
    me = me_block * n_tp + tp
    small = total <= 16
    row_dev, width = x.shape
    part = row_dev // n_tp
    half = wgv.shape[1] // n_tp
    att_rows = qv.shape[0]

    def peer(index):
        return {
            "ep": lax.div(index, quad),
            "role": lax.rem(lax.div(index, n_tp), n_role),
            "tp": lax.rem(index, n_tp),
        }

    def each(start, stop, step):
        def run(k, carry):
            step(k)
            return carry

        lax.fori_loop(start, stop, run, 0, unroll=small)

    barrier = pltpu.get_barrier_semaphore()

    def greet(k):
        pl.semaphore_signal(
            barrier, inc=1, device_id=peer(lax.rem(me + k, total)), device_id_type=MESH
        )

    each(1, total, greet)

    own = pltpu.make_async_copy(x, rows.at[me_block], load_sem.at[0])
    loads = [
        pltpu.make_async_copy(source, target, load_sem.at[1 + i])
        for i, (source, target) in enumerate(
            [(query, qv), (cache, cv), (wg, wgv), (wu, wuv), (wd, wdv)]
        )
    ]
    own.start()
    for load in loads:
        load.start()

    own.wait()
    pl.semaphore_wait(barrier, total - 1)

    def dispatch(block, source):
        return pltpu.make_async_remote_copy(
            src_ref=rows.at[me_block],
            dst_ref=rows.at[source],
            send_sem=d_send.at[block],
            recv_sem=d_recv.at[source],
            device_id=peer(block * n_tp + tp),
            device_id_type=MESH,
        )

    half_ep = n_ep // 2
    near = lax.div(ep, half_ep) * half_ep
    far = lax.rem(near + half_ep, n_ep)

    def near_block(k):
        return near * n_role + lax.rem(me_block - near * n_role + k, half_ep * n_role)

    def far_ep(k):
        return far + lax.rem(ep - near + k, half_ep)

    def relay(source_ep, target, j):
        block = source_ep * n_role + lax.rem(role + j, n_role) if j else source_ep * n_role + role
        return pltpu.make_async_remote_copy(
            src_ref=rows.at[block],
            dst_ref=rows.at[block],
            send_sem=f_send.at[source_ep * n_role + target],
            recv_sem=d_recv.at[block],
            device_id={"role": target},
            device_id_type=MESH,
        )

    each(0, half_ep, lambda k: dispatch(far_ep(k) * n_role + role, me_block).start())
    each(1, half_ep * n_role, lambda k: dispatch(near_block(k), me_block).start())

    def pass_on(k):
        source = far_ep(k)
        dispatch(me_block, source * n_role + role).wait_recv()
        for j in range(1, n_role):
            relay(source, lax.rem(role + j, n_role), 0).start()

    def attend(r):
        q, entries = qv[r], cv[r]
        scores = (
            jnp.dot(q, entries, preferred_element_type=jnp.float32) * score_scale
        )
        visible = lax.broadcasted_iota(jnp.int32, scores.shape, 1) < lens[r]
        scores = jnp.where(visible, scores, -1e30)
        weights = jnp.exp(scores - jnp.max(scores, axis=1, keepdims=True))
        chances = (weights / jnp.sum(weights, axis=1, keepdims=True)).astype(jnp.bfloat16)
        attv[r] = lax.dot_general(
            chances, entries[:LAT], (((1,), (1,)), ((), ())), preferred_element_type=jnp.float32
        ).astype(jnp.bfloat16)

    def put(r):
        return pltpu.make_async_copy(attv.at[r], att.at[r], put_sem.at[r])

    loads[0].wait()
    loads[1].wait()
    cut = att_rows // 2
    for r in range(cut):
        attend(r)
        put(r).start()
        if r == 0:
            each(0, half_ep, pass_on)

    loads[2].wait()
    loads[3].wait()
    each(1, half_ep * n_role, lambda k: dispatch(me_block, near_block(k)).wait_recv())

    count = half_ep * n_role
    lot = count * row_dev

    def gather(first):
        got = rows[pl.ds(first * n_role, count)]
        return got.astype(jnp.float32).reshape(lot, width).astype(jnp.bfloat16)

    def column_sums(gathered, which):
        columns = pl.ds(pl.multiple_of(which * half, half), half)
        gate = jnp.dot(gathered, wgv[:, columns], preferred_element_type=jnp.float32)
        up = jnp.dot(gathered, wuv[:, columns], preferred_element_type=jnp.float32)
        return gate, up

    early = gather(near)
    gate, up = column_sums(early, 1 - tp)
    psend[0, :lot] = gate
    psend[1, :lot] = up
    near_gate, near_up = column_sums(early, tp)

    def relayed(k):
        for j in range(1, n_role):
            relay(far_ep(k), role, j).wait_recv()

    each(0, half_ep, relayed)

    late = gather(far)
    gate, up = column_sums(late, 1 - tp)
    psend[0, lot:] = gate
    psend[1, lot:] = up
    swap = pltpu.make_async_remote_copy(
        src_ref=psend,
        dst_ref=precv,
        send_sem=p_sem.at[0],
        recv_sem=p_sem.at[1],
        device_id={"tp": 1 - tp},
        device_id_type=MESH,
    )
    swap.start()
    gate, up = column_sums(late, tp)
    swap.wait_recv()
    gate = jnp.concatenate([near_gate, gate], axis=0) + precv[0]
    up = jnp.concatenate([near_up, up], axis=0) + precv[1]
    hid[me_quad] = (gate / (1.0 + jnp.exp(-gate)) * up).astype(jnp.bfloat16)

    def share(target, source):
        return pltpu.make_async_remote_copy(
            src_ref=hid.at[me_quad],
            dst_ref=hid.at[source],
            send_sem=h_send.at[target],
            recv_sem=h_recv.at[source],
            device_id={"role": lax.div(target, n_tp), "tp": lax.rem(target, n_tp)},
            device_id_type=MESH,
        )

    for k in range(1, quad):
        share(lax.rem(me_quad + k, quad), me_quad).start()

    for r in range(cut, att_rows):
        attend(r)
        put(r).start()

    loads[4].wait()
    produced = None
    for k in range(quad):
        source = lax.rem(me_quad + k, quad)
        if k:
            share(me_quad, source).wait_recv()
        span = pl.ds(pl.multiple_of(source * half, half), half)
        term = jnp.dot(hid[source], wdv[span, :], preferred_element_type=jnp.float32)
        produced = term if produced is None else produced + term

    produced = produced.reshape(total, part, produced.shape[1]).astype(jnp.bfloat16)
    outb[pl.ds(near * quad, total // 2)] = produced[: total // 2]
    outb[pl.ds(far * quad, total // 2)] = produced[total // 2 :]

    def give(target, source):
        return pltpu.make_async_remote_copy(
            src_ref=outb.at[target],
            dst_ref=ret.at[source],
            send_sem=r_send.at[target],
            recv_sem=r_recv.at[source],
            device_id=peer(target),
            device_id_type=MESH,
        )

    each(1, total, lambda k: give(lax.rem(me + k, total), me).start())
    keep = pltpu.make_async_copy(outb.at[me], ret.at[me], load_sem.at[0])
    keep.start()

    named, score = ids[...], gates[...]
    mine = lax.broadcasted_iota(jnp.int32, (part, row_dev), 1) == tp * part + (
        lax.broadcasted_iota(jnp.int32, (part, row_dev), 0)
    )
    table = []
    for e in range(n_ep):
        weight = jnp.sum(jnp.where(named == e, score, 0.0), axis=0, keepdims=True)
        table.append(jnp.sum(jnp.where(mine, weight, 0.0), axis=1, keepdims=True))

    keep.wait()
    each(1, total, lambda k: give(me, lax.rem(me + k, total)).wait_recv())

    columns = ret.shape[2]
    for j in range(quad):
        acc = None
        for e in range(n_ep):
            term = table[e] * ret[e * quad + j].astype(jnp.float32)
            acc = term if acc is None else acc + term
        moev[:, j * columns : (j + 1) * columns] = acc.astype(jnp.bfloat16)
    last = pltpu.make_async_copy(moev, moe, load_sem.at[1])
    last.start()

    each(0, half_ep, lambda k: dispatch(far_ep(k) * n_role + role, me_block).wait_send())
    each(1, half_ep * n_role, lambda k: dispatch(near_block(k), me_block).wait_send())

    def sent(k):
        for j in range(1, n_role):
            relay(far_ep(k), lax.rem(role + j, n_role), 0).wait_send()

    each(0, half_ep, sent)
    swap.wait_send()
    for k in range(1, quad):
        share(lax.rem(me_quad + k, quad), me_quad).wait_send()
    each(1, total, lambda k: give(lax.rem(me + k, total), me).wait_send())
    for r in range(att_rows):
        put(r).wait()
    last.wait()


def shards(sizes, moe_in, expert_ids, gate_scores, w_gate, w_up, w_down, att_query, att_cache, cache_len):
    n_ep, n_role, n_tp = sizes
    quad, blocks = n_role * n_tp, n_ep * n_role
    total = blocks * n_tp
    row_dev, width = moe_in.shape
    part = row_dev // n_tp
    hidden = w_gate.shape[2]
    units, columns = w_down.shape[1:]
    half = hidden // n_tp
    att_rows, heads, _ = att_query.shape
    entries = jnp.swapaxes(att_cache, 1, 2)
    bf16, f32 = jnp.bfloat16, jnp.float32
    anywhere = pl.BlockSpec(memory_space=pl.ANY)
    vmem = pl.BlockSpec(memory_space=pltpu.VMEM)
    smem = pl.BlockSpec(memory_space=pltpu.SMEM)
    dma = pltpu.SemaphoreType.DMA
    flops = 2 * blocks * row_dev * (2 * width * hidden + units * columns)
    moe, att = pl.pallas_call(
        functools.partial(body, sizes),
        out_shape=(
            jax.ShapeDtypeStruct((part, columns * quad), bf16),
            jax.ShapeDtypeStruct((att_rows, heads, LAT), bf16),
        ),
        in_specs=[anywhere, vmem, vmem] + [anywhere] * 5 + [smem],
        out_specs=(anywhere, anywhere),
        scratch_shapes=[
            pltpu.VMEM((blocks, row_dev, width), bf16),
            pltpu.VMEM((width, hidden), bf16),
            pltpu.VMEM((width, hidden), bf16),
            pltpu.VMEM((units, columns), bf16),
            pltpu.VMEM(att_query.shape, bf16),
            pltpu.VMEM(entries.shape, bf16),
            pltpu.VMEM((2, blocks * row_dev, half), f32),
            pltpu.VMEM((2, blocks * row_dev, half), f32),
            pltpu.VMEM((quad, blocks * row_dev, half), bf16),
            pltpu.VMEM((total, part, columns), bf16),
            pltpu.VMEM((total, part, columns), bf16),
            pltpu.VMEM((att_rows, heads, LAT), bf16),
            pltpu.VMEM((part, columns * quad), bf16),
            dma((6,)),
            dma((att_rows,)),
            dma((blocks,)),
            dma((blocks,)),
            dma((blocks,)),
            dma((2,)),
            dma((quad,)),
            dma((quad,)),
            dma((total,)),
            dma((total,)),
        ],
        compiler_params=pltpu.CompilerParams(
            collective_id=0, has_side_effects=True, vmem_limit_bytes=56 * 1024 * 1024
        ),
        cost_estimate=pl.CostEstimate(flops=flops, bytes_accessed=8 << 20, transcendentals=0),
    )(
        moe_in, expert_ids.T, gate_scores.T, w_gate[0], w_up[0], w_down[0], att_query, entries, cache_len
    )
    return settled(moe, att)


def settle(a, b, out_a, out_b, held_a, held_b, sem):
    rows = b.shape[0]
    inward = [pltpu.make_async_copy(a, held_a, sem.at[0, 0])]
    outward = [pltpu.make_async_copy(held_a, out_a, sem.at[1, 0])]
    for r in range(rows):
        inward.append(pltpu.make_async_copy(b.at[r], held_b.at[r], sem.at[0, 1 + r]))
        outward.append(pltpu.make_async_copy(held_b.at[r], out_b.at[r], sem.at[1, 1 + r]))
    for copy in inward:
        copy.start()
    for copy, onward in zip(inward, outward):
        copy.wait()
        onward.start()
    for onward in outward:
        onward.wait()


def settled(a, b):
    anywhere = pl.BlockSpec(memory_space=pl.ANY)
    return pl.pallas_call(
        settle,
        out_shape=(jax.ShapeDtypeStruct(a.shape, a.dtype), jax.ShapeDtypeStruct(b.shape, b.dtype)),
        in_specs=[anywhere, anywhere],
        out_specs=(anywhere, anywhere),
        scratch_shapes=[
            pltpu.VMEM(a.shape, a.dtype),
            pltpu.VMEM(b.shape, b.dtype),
            pltpu.SemaphoreType.DMA((2, 1 + b.shape[0])),
        ],
        compiler_params=pltpu.CompilerParams(vmem_limit_bytes=56 * 1024 * 1024),
    )(a, b)


def solution(mesh):
    placed = (
        P(("groups", "ep", "role"), "tp"),
        P(("groups", "ep", "role"), None),
        P(("groups", "ep", "role"), None),
        P("ep", "tp", "role"),
        P("ep", "tp", "role"),
        P("ep", None, ("role", "tp")),
        P(("groups", "ep", "role"), "tp", None),
        P(("groups", "ep", "role"), None, None),
        P(("groups", "ep", "role")),
    )
    sizes = (mesh.shape["ep"], mesh.shape["role"], mesh.shape["tp"])
    return jax.shard_map(
        functools.partial(shards, sizes),
        mesh=mesh,
        in_specs=placed,
        out_specs=(
            P(("groups", "ep", "role", "tp"), None),
            P(("groups", "ep", "role"), "tp", None),
        ),
        check_vma=False,
    )
```
